32 devices in a mesh: row: 16 (over z, x, core), col: 2 (over y).
Axes of the slice: x: 2, y: 2, z: 4, core: 2. Of those that a mesh axis runs over, the one named last changes fastest.
Arguments:
- coefficients: float32 [2, 1, 256, 256, 256], P(None, None, 'col', 'row'), may hold values from -6 to 6
- real_bands: float32 [2, 256, 256, 256], P(None, 'col', 'row'), may hold values from -6 to 6
Outputs:
- spline_coefs: float32 [2, 1, 256, 256, 256], P(None, None, None, ('row', 'col'))
- spline_table: float32 [2, 256, 256, 256], P('col', 'row')
The draws below stay inside these ranges and needn't reach their ends.
All inputs are finite; a program needn't handle non-finite values.
Results may differ from the reference program's by a relative error of at most 0.00007.
Values sent between devices are 32-bit elements; how exact they have to be, the bound alone decides.
A program may use at most 64 MiB of HBM per device.

```python
import jax
import jax.numpy as jnp
from jax import lax

NX = 256
NY = 256
NZ = 256
NB = 1
NA = 2


def block_levels(own_key, extent, split, low, top_value):
    def one(axis_at, parts):
        draws = jax.random.uniform(jax.random.fold_in(jax.random.fold_in(own_key, 6), axis_at), (parts,), jnp.float32, low / len(split), top_value / len(split))
        return jnp.repeat(jnp.exp(draws), extent[axis_at] // parts).reshape((-1,) + (1,) * (len(extent) - axis_at - 1))

    gain = one(*split[0])
    for cut in split[1:]:
        gain = gain * one(*cut)
    return gain


def noise(own_key, dims, deviation, bound, split=(), kind=jnp.bfloat16):
    drawn = jax.random.normal(own_key, dims, jnp.float32) * deviation
    if len(split) > 0:
        drawn = block_levels(own_key, dims, split, -0.22, 0.18) * drawn
    return jnp.clip(drawn, min=-bound, max=bound).astype(kind)


def setup_inputs(seed: int = 0) -> dict:
    streams_of = jax.random.split(jax.random.key(seed), 3)
    return {
        "coefficients": noise(streams_of[0], (2, NB, NZ, NY, NX), 1.0, 6.0, ((2, 2), (3, 16)), jnp.float32),
        "real_bands": noise(streams_of[1], (NA, NZ, NY, NX), 1.0, 6.0, ((1, 2), (2, 16)), jnp.float32),
    }


def prefilter(length, dtype):
    angle = (2.0 * jnp.pi / length) * jnp.arange(length).astype(dtype)
    return (4.0 + 2.0 * jnp.cos(angle)) / 6.0


def reference(coefficients, real_bands):
    dtype = coefficients.dtype
    scale = prefilter(NZ, dtype)[:, None, None] * prefilter(NY, dtype)[None, :, None] * prefilter(NX, dtype)[None, None, :]

    def one_band(pair):
        spectrum = (pair[0] + 1j * pair[1]) / scale
        field = jnp.fft.ifftn(spectrum, axes=(0, 1, 2), norm="ortho")
        field = jnp.transpose(field, (0, 2, 1))
        return jnp.stack([jnp.real(field), jnp.imag(field)]).astype(dtype)

    moved = lax.map(one_band, (coefficients[0], coefficients[1]))
    spline_coefs = jnp.transpose(moved, (1, 0, 2, 3, 4))
    spline_table = jnp.transpose(real_bands, (0, 3, 2, 1))
    return spline_coefs, spline_table
```

```python
import math

import jax
import jax.numpy as jnp
import numpy as np
from jax import lax
from jax.sharding import PartitionSpec as P

precision = lax.Precision.HIGH
axes = ("row", "col")


def transform_table(length):
    counter = np.arange(length)
    angle = (counter[:, None] * counter[None, :] % length) * (2.0 * math.pi / length)
    weight = 6.0 / ((4.0 + 2.0 * np.cos(counter * (2.0 * math.pi / length))) * math.sqrt(length))
    cosine = np.cos(angle) * weight[:, None]
    sine = np.sin(angle) * weight[:, None]
    table = np.stack([np.stack([cosine, sine], 1), np.stack([-sine, cosine], 1)])
    return table.astype(np.float32)


def local(coefficients, real_bands):
    rows = lax.axis_size("row")
    cols = lax.axis_size("col")
    devices = rows * cols
    _, bands, z_local, y_local, x_full = coefficients.shape
    z_full = z_local * cols
    y_full = y_local * rows
    x_final = x_full // devices
    table_bands = real_bands.shape[0] // cols
    x_rows = x_full // rows

    turned = real_bands.reshape(cols, table_bands, z_local, y_local, rows, x_rows)
    turned = jnp.transpose(turned, (4, 0, 1, 5, 3, 2))
    turned = turned.reshape(devices, table_bands, x_rows, y_local, z_local)
    placed = lax.all_to_all(turned, axes, split_axis=0, concat_axis=0, tiled=True)
    placed = placed.reshape(rows, cols, table_bands, x_rows, y_local, z_local)
    spline_table = jnp.transpose(placed, (2, 3, 0, 4, 1, 5)).reshape(table_bands, x_rows, y_full, z_full)

    x_table = transform_table(x_full).reshape(2, x_full, 2, devices, x_final)
    z_table = transform_table(z_full).reshape(2, cols, z_local, 2, z_full)
    y_table = transform_table(y_full).reshape(2, rows, y_local, 2, y_full)
    first = jnp.einsum("cbzyk,ckedq->debyqz", coefficients, x_table, precision=precision)
    moved = lax.all_to_all(first, axes, split_axis=0, concat_axis=0, tiled=True)
    moved = moved.reshape(rows, cols, 2, bands, y_local, x_final, z_local)
    second = jnp.einsum("rjebyqz,ejzfn->fbnqry", moved, z_table, precision=precision)
    spline_coefs = jnp.einsum("fbnqry,fryhk->hbnqk", second, y_table, precision=precision)
    return spline_coefs, spline_table


def solution(mesh):
    placed = (P(None, None, "col", "row", None), P(None, "col", "row", None))
    return jax.shard_map(
        local,
        mesh=mesh,
        in_specs=placed,
        out_specs=(P(None, None, None, ("row", "col"), None), P("col", "row", None, None)),
        check_vma=False,
    )
```

```python
import functools
import math

import jax
import jax.numpy as jnp
import ml_dtypes
import numpy as np
from jax import lax
from jax.experimental import pallas as pl
from jax.experimental.pallas import tpu as pltpu
from jax.sharding import PartitionSpec as P

precision = lax.Precision.HIGH
axes = ("row", "col")
MESH = pl.DeviceIdType.MESH
LANES = 128
SUBLANES = 8


def transform_table(length):
    counter = np.arange(length)
    angle = (counter[:, None] * counter[None, :] % length) * (2.0 * math.pi / length)
    weight = 6.0 / ((4.0 + 2.0 * np.cos(counter * (2.0 * math.pi / length))) * math.sqrt(length))
    cosine = np.cos(angle) * weight[:, None]
    sine = np.sin(angle) * weight[:, None]
    table = np.stack([np.stack([cosine, sine], 1), np.stack([-sine, cosine], 1)])
    return table.astype(np.float32)


def split_table(table):
    high = table.astype(ml_dtypes.bfloat16)
    low = (table - high.astype(np.float32)).astype(ml_dtypes.bfloat16)
    return np.stack([high, low])


def split(values):
    high = values.astype(jnp.bfloat16)
    return high, (values - high.astype(jnp.float32)).astype(jnp.bfloat16)


def product(left, right, contract):
    def one(a, b):
        return lax.dot_general(a, b, (contract, ((), ())), preferred_element_type=jnp.float32)

    return one(left[0], right[0]) + (one(left[0], right[1]) + one(left[1], right[0]))


def kernel(
    rows, cols, y_local,
    coefficients, bands, x_table, z_table, y_table,
    out, table_out,
    source, band_in, x_parts, z_parts, y_parts, turned, first, arrived, result,
    load_sem, local_sem, first_send, first_recv, band_send, band_recv,
):
    row, col = lax.axis_index("row"), lax.axis_index("col")
    half_rows = rows // 2
    half, place = row // half_rows, row % half_rows
    x_tiles, y_tiles = source.shape[1], result.shape[1]
    x_full = x_tiles * LANES
    x_rows = x_full // rows
    y_full = y_local * rows
    z_full = LANES * cols
    block = y_local * SUBLANES

    def target(by_col, by_half, step):
        to_row = (half + by_half) % 2 * half_rows + (place + step) % half_rows
        return to_row, (col + by_col) % cols

    def origin(by_col, by_half, step):
        from_row = (half + by_half) % 2 * half_rows + (place - step + half_rows) % half_rows
        return from_row, (col - by_col + cols) % cols

    def number(by_col, by_half, step):
        return (by_col * 2 + by_half) * half_rows + step

    groups = [(by_col, by_half) for by_half in (1, 0) for by_col in range(cols)]

    def each_step(group, do):
        own = group == (0, 0)

        def body(step, _):
            do(*group, step)
            return 0

        lax.fori_loop(1 if own else 0, half_rows, body, 0)

    barrier = pltpu.get_barrier_semaphore()

    def greet(by_col, by_half, step):
        pl.semaphore_signal(barrier, inc=1, device_id=target(by_col, by_half, step), device_id_type=MESH)

    for group in groups:
        each_step(group, greet)

    def load(k, src, dst):
        return pltpu.make_async_copy(src, dst, load_sem.at[k])

    def load_band(b, tile):
        return load(b * x_tiles + tile, bands.at[b, :, pl.ds(tile * LANES, LANES)], band_in.at[b, tile])

    k = cols * x_tiles
    loads = [
        load(k, x_table, x_parts),
        load(k + 1, z_table, z_parts),
        load(k + 2, y_table, y_parts),
    ]
    for tile in range(x_tiles):
        loads.append(load(k + 3 + tile, coefficients.at[:, :, pl.ds(tile * LANES, LANES)], source.at[:, tile]))
    for by_col in range(cols):
        for tile in range(x_tiles):
            load_band((col + by_col) % cols, tile).start()
    for one in loads:
        one.start()

    def turn(by_col, by_half):
        b = (col + by_col) % cols
        half_tiles = x_tiles // 2
        lead = (half + by_half) % 2 * half_tiles
        flat = turned.reshape(cols, x_full * y_local, LANES)

        def body(y, _):
            for at in range(half_tiles):
                plane = band_in[b, lead + at, pl.ds(y, LANES, stride=y_local), :]
                flat[b, pl.ds((lead + at) * LANES * y_local + y, LANES, stride=y_local), :] = plane.T
            return 0

        lax.fori_loop(0, y_local, body, 0)

    def band_copy(by_col, by_half, step, place_row, place_col):
        k = number(by_col, by_half, step)
        to_row, to_col = target(by_col, by_half, step)
        return pltpu.make_async_remote_copy(
            src_ref=turned.at[to_col, pl.ds(to_row * x_rows, x_rows)],
            dst_ref=table_out.at[
                :,
                pl.ds(pl.multiple_of(place_row * y_local, SUBLANES), y_local),
                pl.ds(pl.multiple_of(place_col * LANES, LANES), LANES),
            ],
            send_sem=band_send.at[k],
            recv_sem=band_recv.at[k],
            device_id=(to_row, to_col),
            device_id_type=MESH,
        )

    def first_copy(by_col, by_half, step, place_row, place_col):
        k = number(by_col, by_half, step)
        to_row, to_col = target(by_col, by_half, step)
        return pltpu.make_async_remote_copy(
            src_ref=first.at[to_row * cols + to_col],
            dst_ref=arrived.at[place_col, :, pl.ds(pl.multiple_of(place_row * block, SUBLANES), block)],
            send_sem=first_send.at[k],
            recv_sem=first_recv.at[k],
            device_id=(to_row, to_col),
            device_id_type=MESH,
        )

    def send_band(by_col, by_half, step):
        band_copy(by_col, by_half, step, row, col).start()

    for tile in range(x_tiles):
        load_band(col, tile).wait()
    turn(0, 1)
    pl.semaphore_wait(barrier, rows * cols - 1)
    each_step((0, 1), send_band)

    for one in loads:
        one.wait()

    def x_step(pair, _):
        y = pair * 2
        parts = []
        for part in range(2):
            for tile in range(x_tiles):
                lines = [source[part, tile, pl.ds(y + j, LANES, stride=y_local), :] for j in range(2)]
                parts.append(jnp.concatenate(lines, axis=0))
        lines = split(jnp.concatenate(parts, axis=1))
        made = product((x_parts[0], x_parts[1]), lines, ((1,), (1,)))
        for part in range(2):
            for j in range(2):
                piece = made[part * x_full : (part + 1) * x_full, j * LANES : (j + 1) * LANES]
                at = pl.multiple_of((y + j) * SUBLANES, SUBLANES)
                first[:, part, pl.ds(at, SUBLANES), :] = piece.reshape(rows * cols, SUBLANES, LANES)
        return 0

    lax.fori_loop(0, y_local // 2, x_step, 0)

    def send_first(step, _):
        for group in groups:
            if group == (0, 0):

                @pl.when(step > 0)
                def _():
                    first_copy(*group, step, row, col).start()

            else:
                first_copy(*group, step, row, col).start()
        return 0

    lax.fori_loop(0, half_rows, send_first, 0)
    own_first = pltpu.make_async_copy(
        first.at[row * cols + col],
        arrived.at[col, :, pl.ds(pl.multiple_of(row * block, SUBLANES), block)],
        local_sem.at[0],
    )
    own_first.start()

    for by_col in range(1, cols):
        for tile in range(x_tiles):
            load_band((col + by_col) % cols, tile).wait()
    for group in groups:
        if group != (0, 1):
            turn(*group)
            each_step(group, send_band)
    own_band = pltpu.make_async_copy(
        turned.at[col, pl.ds(row * x_rows, x_rows)],
        table_out.at[
            :,
            pl.ds(pl.multiple_of(row * y_local, SUBLANES), y_local),
            pl.ds(pl.multiple_of(col * LANES, LANES), LANES),
        ],
        local_sem.at[1],
    )
    own_band.start()

    own_first.wait()
    for group in groups:
        each_step(group, lambda *at: first_copy(*at, *origin(*at)).wait_recv())

    def final_step(x, _):
        pieces = [
            arrived[c, part, pl.ds(x, y_full, stride=SUBLANES), :] for part in range(2) for c in range(cols)
        ]
        lines = split(jnp.concatenate(pieces, axis=1))
        second = product((z_parts[0], z_parts[1]), lines, ((1,), (1,)))
        lines = split(jnp.concatenate([second[:z_full], second[z_full:]], axis=1))
        third = product(lines, (y_parts[0], y_parts[1]), ((1,), (0,)))
        for part in range(2):
            for tile in range(y_tiles):
                at = part * y_full + tile * LANES
                result[part, tile, pl.ds(x, z_full, stride=SUBLANES), :] = third[:, at : at + LANES]
        return 0

    lax.fori_loop(0, SUBLANES, final_step, 0)
    stores = [
        pltpu.make_async_copy(result.at[:, tile], out.at[:, :, pl.ds(tile * LANES, LANES)], local_sem.at[2 + tile])
        for tile in range(y_tiles)
    ]
    for store in stores:
        store.start()
    for store in stores:
        store.wait()
    own_band.wait()
    for group in groups:
        each_step(group, lambda *at: first_copy(*at, *origin(*at)).wait_send())
        each_step(group, lambda *at: band_copy(*at, *origin(*at)).wait_send())
        each_step(group, lambda *at: band_copy(*at, *origin(*at)).wait_recv())


def fused(coefficients, real_bands, rows, cols):
    _, _, z_local, y_local, x_full = coefficients.shape
    z_full, y_full, devices = z_local * cols, y_local * rows, rows * cols
    x_rows = x_full // rows
    x_table = split_table(np.transpose(transform_table(x_full), (2, 3, 0, 1)).reshape(2 * x_full, 2 * x_full))
    z_table = split_table(np.transpose(transform_table(z_full), (2, 3, 0, 1)).reshape(2 * z_full, 2 * z_full))
    y_table = split_table(transform_table(y_full).reshape(2 * y_full, 2 * y_full))
    flops = 3 * 2 * 2 * 2 * (x_full + y_full + z_full) * coefficients.size
    out, table = pl.pallas_call(
        functools.partial(kernel, rows, cols, y_local),
        out_shape=[
            jax.ShapeDtypeStruct((2, z_full * SUBLANES, y_full), jnp.float32),
            jax.ShapeDtypeStruct((x_rows, y_full, z_full), jnp.float32),
        ],
        in_specs=[pl.BlockSpec(memory_space=pl.ANY)] * 5,
        out_specs=[pl.BlockSpec(memory_space=pl.ANY)] * 2,
        scratch_shapes=[
            pltpu.VMEM((2, x_full // LANES, z_local * y_local, LANES), jnp.float32),
            pltpu.VMEM((cols, x_full // LANES, z_local * y_local, LANES), jnp.float32),
            pltpu.VMEM(x_table.shape, jnp.bfloat16),
            pltpu.VMEM(z_table.shape, jnp.bfloat16),
            pltpu.VMEM(y_table.shape, jnp.bfloat16),
            pltpu.VMEM((cols, x_full, y_local, LANES), jnp.float32),
            pltpu.VMEM((devices, 2, y_local * SUBLANES, LANES), jnp.float32),
            pltpu.VMEM((cols, 2, y_full * SUBLANES, LANES), jnp.float32),
            pltpu.VMEM((2, y_full // LANES, z_full * SUBLANES, LANES), jnp.float32),
            pltpu.SemaphoreType.DMA(((cols + 1) * (x_full // LANES) + 3,)),
            pltpu.SemaphoreType.DMA((2 + y_full // LANES,)),
            pltpu.SemaphoreType.DMA((devices,)),
            pltpu.SemaphoreType.DMA((devices,)),
            pltpu.SemaphoreType.DMA((devices,)),
            pltpu.SemaphoreType.DMA((devices,)),
        ],
        compiler_params=pltpu.CompilerParams(
            collective_id=0, has_side_effects=True, vmem_limit_bytes=56 * 1024 * 1024
        ),
        cost_estimate=pl.CostEstimate(flops=flops, bytes_accessed=16 * coefficients.size, transcendentals=0),
    )(
        coefficients.reshape(2, z_local * y_local, x_full),
        real_bands.reshape(cols, z_local * y_local, x_full),
        jnp.asarray(x_table),
        jnp.asarray(z_table),
        jnp.asarray(y_table),
    )
    return out.reshape(2, 1, z_full, SUBLANES, y_full), table[None]


def local(coefficients, real_bands):
    rows = lax.axis_size("row")
    cols = lax.axis_size("col")
    _, bands, z_local, y_local, x_full = coefficients.shape
    fits = (
        bands == 1
        and real_bands.shape[0] == cols
        and z_local == LANES
        and y_local % (2 * SUBLANES) == 0
        and x_full == SUBLANES * rows * cols
        and x_full % (2 * LANES) == 0
        and rows % 2 == 0
    )
    if fits:
        return fused(coefficients, real_bands, rows, cols)
    return general(coefficients, real_bands)


def general(coefficients, real_bands):
    rows = lax.axis_size("row")
    cols = lax.axis_size("col")
    devices = rows * cols
    _, bands, z_local, y_local, x_full = coefficients.shape
    z_full = z_local * cols
    y_full = y_local * rows
    x_final = x_full // devices
    table_bands = real_bands.shape[0] // cols
    x_rows = x_full // rows

    turned = real_bands.reshape(cols, table_bands, z_local, y_local, rows, x_rows)
    turned = jnp.transpose(turned, (4, 0, 1, 5, 3, 2))
    turned = turned.reshape(devices, table_bands, x_rows, y_local, z_local)
    placed = lax.all_to_all(turned, axes, split_axis=0, concat_axis=0, tiled=True)
    placed = placed.reshape(rows, cols, table_bands, x_rows, y_local, z_local)
    spline_table = jnp.transpose(placed, (2, 3, 0, 4, 1, 5)).reshape(table_bands, x_rows, y_full, z_full)

    x_table = transform_table(x_full).reshape(2, x_full, 2, devices, x_final)
    z_table = transform_table(z_full).reshape(2, cols, z_local, 2, z_full)
    y_table = transform_table(y_full).reshape(2, rows, y_local, 2, y_full)
    first = jnp.einsum("cbzyk,ckedq->debyqz", coefficients, x_table, precision=precision)
    moved = lax.all_to_all(first, axes, split_axis=0, concat_axis=0, tiled=True)
    moved = moved.reshape(rows, cols, 2, bands, y_local, x_final, z_local)
    second = jnp.einsum("rjebyqz,ejzfn->fbnqry", moved, z_table, precision=precision)
    spline_coefs = jnp.einsum("fbnqry,fryhk->hbnqk", second, y_table, precision=precision)
    return spline_coefs, spline_table


def solution(mesh):
    placed = (P(None, None, "col", "row", None), P(None, "col", "row", None))
    return jax.shard_map(
        local,
        mesh=mesh,
        in_specs=placed,
        out_specs=(P(None, None, None, ("row", "col"), None), P("col", "row", None, None)),
        check_vma=False,
    )
```

```python
import functools
import math

import jax
import jax.numpy as jnp
import ml_dtypes
import numpy as np
from jax import lax
from jax.experimental import pallas as pl
from jax.experimental.pallas import tpu as pltpu
from jax.sharding import PartitionSpec as P

precision = lax.Precision.HIGH
axes = ("row", "col")
MESH = pl.DeviceIdType.MESH
LANES = 128
SUBLANES = 8


def transform_table(length):
    counter = np.arange(length)
    angle = (counter[:, None] * counter[None, :] % length) * (2.0 * math.pi / length)
    weight = 6.0 / ((4.0 + 2.0 * np.cos(counter * (2.0 * math.pi / length))) * math.sqrt(length))
    cosine = np.cos(angle) * weight[:, None]
    sine = np.sin(angle) * weight[:, None]
    table = np.stack([np.stack([cosine, sine], 1), np.stack([-sine, cosine], 1)])
    return table.astype(np.float32)


def split_table(table):
    high = table.astype(ml_dtypes.bfloat16)
    low = (table - high.astype(np.float32)).astype(ml_dtypes.bfloat16)
    return np.stack([high, low])


def split(values):
    high = values.astype(jnp.bfloat16)
    return high, (values - high.astype(jnp.float32)).astype(jnp.bfloat16)


def product(left, right, contract):
    def one(a, b):
        return lax.dot_general(a, b, (contract, ((), ())), preferred_element_type=jnp.float32)

    return one(left[0], right[0]) + (one(left[0], right[1]) + one(left[1], right[0]))


def kernel(
    rows, cols, y_local,
    coefficients, bands, x_table, z_table, y_table,
    out, table_out,
    source, band_in, x_parts, z_parts, y_parts, turned, first, arrived, result,
    load_sem, local_sem, first_send, first_recv, band_send, band_recv,
):
    row, col = lax.axis_index("row"), lax.axis_index("col")
    half_rows = rows // 2
    half, place = row // half_rows, row % half_rows
    x_tiles, y_tiles = source.shape[1], result.shape[1]
    x_full = x_tiles * LANES
    x_rows = x_full // rows
    y_full = y_local * rows
    z_full = LANES * cols
    block = y_local * SUBLANES

    def target(by_col, by_half, step):
        to_row = (half + by_half) % 2 * half_rows + (place + step) % half_rows
        return to_row, (col + by_col) % cols

    def origin(by_col, by_half, step):
        from_row = (half + by_half) % 2 * half_rows + (place - step + half_rows) % half_rows
        return from_row, (col - by_col + cols) % cols

    def number(by_col, by_half, step):
        return (by_col * 2 + by_half) * half_rows + step

    groups = [(by_col, by_half) for by_col in range(cols) for by_half in (1, 0)]

    def each_step(chosen, do):
        def body(step, _):
            for group in chosen:
                if group == (0, 0):
                    pl.when(step > 0)(functools.partial(do, *group, step))
                else:
                    do(*group, step)
            return 0

        lax.fori_loop(0, half_rows, body, 0)

    barrier = pltpu.get_barrier_semaphore()

    def greet(by_col, by_half, step):
        pl.semaphore_signal(barrier, inc=1, device_id=target(by_col, by_half, step), device_id_type=MESH)

    each_step(groups, greet)

    def load(k, src, dst):
        return pltpu.make_async_copy(src, dst, load_sem.at[k])

    half_tiles = x_tiles // 2

    def lead(by_half):
        return (half + by_half) % 2 * half_tiles

    def load_bands(by_col, by_half):
        b = (col + by_col) % cols
        made = []
        for at in range(half_tiles):
            tile = lead(by_half) + at
            lanes = pl.ds(pl.multiple_of(tile * LANES, LANES), LANES)
            made.append(load((by_col * 2 + by_half) * half_tiles + at, bands.at[b, :, lanes], band_in.at[b, tile]))
        return made

    k = cols * x_tiles
    loads = [
        load(k, x_table, x_parts),
        load(k + 1, z_table, z_parts),
        load(k + 2, y_table, y_parts),
    ]
    for tile in range(x_tiles):
        loads.append(load(k + 3 + tile, coefficients.at[:, :, pl.ds(tile * LANES, LANES)], source.at[:, tile]))
    for group in groups[:2]:
        for one in load_bands(*group):
            one.start()
    for one in loads:
        one.start()
    for group in groups[2:]:
        for one in load_bands(*group):
            one.start()

    def turn(by_col, by_half):
        b = (col + by_col) % cols
        first_tile = lead(by_half)
        flat = turned.reshape(cols, x_full * y_local, LANES)

        def body(y, _):
            for at in range(half_tiles):
                plane = band_in[b, first_tile + at, pl.ds(y, LANES, stride=y_local), :]
                flat[b, pl.ds((first_tile + at) * LANES * y_local + y, LANES, stride=y_local), :] = plane.T
            return 0

        lax.fori_loop(0, y_local, body, 0)

    def band_copy(by_col, by_half, step, place_row, place_col):
        k = number(by_col, by_half, step)
        to_row, to_col = target(by_col, by_half, step)
        return pltpu.make_async_remote_copy(
            src_ref=turned.at[to_col, pl.ds(to_row * x_rows, x_rows)],
            dst_ref=table_out.at[
                :,
                pl.ds(pl.multiple_of(place_row * y_local, SUBLANES), y_local),
                pl.ds(pl.multiple_of(place_col * LANES, LANES), LANES),
            ],
            send_sem=band_send.at[k],
            recv_sem=band_recv.at[k],
            device_id=(to_row, to_col),
            device_id_type=MESH,
        )

    def first_copy(by_col, by_half, step, place_row, place_col):
        k = number(by_col, by_half, step)
        to_row, to_col = target(by_col, by_half, step)
        return pltpu.make_async_remote_copy(
            src_ref=first.at[to_row * cols + to_col],
            dst_ref=arrived.at[place_col, :, pl.ds(pl.multiple_of(place_row * block, SUBLANES), block)],
            send_sem=first_send.at[k],
            recv_sem=first_recv.at[k],
            device_id=(to_row, to_col),
            device_id_type=MESH,
        )

    def send_band(by_col, by_half, step):
        band_copy(by_col, by_half, step, row, col).start()

    for one in load_bands(0, 1):
        one.wait()
    turn(0, 1)
    pl.semaphore_wait(barrier, rows * cols - 1)
    each_step([(0, 1)], send_band)
    for one in load_bands(0, 0):
        one.wait()
    turn(0, 0)
    each_step([(0, 0)], send_band)

    for one in loads:
        one.wait()

    def x_step(pair, _):
        y = pair * 2
        parts = []
        for part in range(2):
            for tile in range(x_tiles):
                lines = [source[part, tile, pl.ds(y + j, LANES, stride=y_local), :] for j in range(2)]
                parts.append(jnp.concatenate(lines, axis=0))
        lines = split(jnp.concatenate(parts, axis=1))
        made = product((x_parts[0], x_parts[1]), lines, ((1,), (1,)))
        for part in range(2):
            for j in range(2):
                piece = made[part * x_full : (part + 1) * x_full, j * LANES : (j + 1) * LANES]
                at = pl.multiple_of((y + j) * SUBLANES, SUBLANES)
                first[:, part, pl.ds(at, SUBLANES), :] = piece.reshape(rows * cols, SUBLANES, LANES)
        return 0

    lax.fori_loop(0, y_local // 2, x_step, 0)

    each_step(groups, lambda *at: first_copy(*at, row, col).start())
    own_first = pltpu.make_async_copy(
        first.at[row * cols + col],
        arrived.at[col, :, pl.ds(pl.multiple_of(row * block, SUBLANES), block)],
        local_sem.at[0],
    )
    own_first.start()

    for group in groups[2:]:
        for one in load_bands(*group):
            one.wait()
        turn(*group)
    each_step(groups[2:], send_band)
    own_band = pltpu.make_async_copy(
        turned.at[col, pl.ds(row * x_rows, x_rows)],
        table_out.at[
            :,
            pl.ds(pl.multiple_of(row * y_local, SUBLANES), y_local),
            pl.ds(pl.multiple_of(col * LANES, LANES), LANES),
        ],
        local_sem.at[1],
    )
    own_band.start()

    own_first.wait()
    each_step(groups, lambda *at: first_copy(*at, *origin(*at)).wait_recv())

    def final_step(x, _):
        pieces = [
            arrived[c, part, pl.ds(x, y_full, stride=SUBLANES), :] for part in range(2) for c in range(cols)
        ]
        lines = split(jnp.concatenate(pieces, axis=1))
        second = product((z_parts[0], z_parts[1]), lines, ((1,), (1,)))
        lines = split(jnp.concatenate([second[:z_full], second[z_full:]], axis=1))
        third = product(lines, (y_parts[0], y_parts[1]), ((1,), (0,)))
        for part in range(2):
            for tile in range(y_tiles):
                at = part * y_full + tile * LANES
                result[part, tile, pl.ds(x, z_full, stride=SUBLANES), :] = third[:, at : at + LANES]
        return 0

    lax.fori_loop(0, SUBLANES, final_step, 0)
    stores = [
        pltpu.make_async_copy(result.at[:, tile], out.at[:, :, pl.ds(tile * LANES, LANES)], local_sem.at[2 + tile])
        for tile in range(y_tiles)
    ]
    for store in stores:
        store.start()
    for store in stores:
        store.wait()
    own_band.wait()
    each_step(groups, lambda *at: first_copy(*at, *origin(*at)).wait_send())
    each_step(groups, lambda *at: band_copy(*at, *origin(*at)).wait_send())
    each_step(groups, lambda *at: band_copy(*at, *origin(*at)).wait_recv())


def fused(coefficients, real_bands, rows, cols):
    _, _, z_local, y_local, x_full = coefficients.shape
    z_full, y_full, devices = z_local * cols, y_local * rows, rows * cols
    x_rows = x_full // rows
    x_table = split_table(np.transpose(transform_table(x_full), (2, 3, 0, 1)).reshape(2 * x_full, 2 * x_full))
    z_table = split_table(np.transpose(transform_table(z_full), (2, 3, 0, 1)).reshape(2 * z_full, 2 * z_full))
    y_table = split_table(transform_table(y_full).reshape(2 * y_full, 2 * y_full))
    flops = 3 * 2 * 2 * 2 * (x_full + y_full + z_full) * coefficients.size
    out, table = pl.pallas_call(
        functools.partial(kernel, rows, cols, y_local),
        out_shape=[
            jax.ShapeDtypeStruct((2, z_full * SUBLANES, y_full), jnp.float32),
            jax.ShapeDtypeStruct((x_rows, y_full, z_full), jnp.float32),
        ],
        in_specs=[pl.BlockSpec(memory_space=pl.ANY)] * 5,
        out_specs=[pl.BlockSpec(memory_space=pl.ANY)] * 2,
        scratch_shapes=[
            pltpu.VMEM((2, x_full // LANES, z_local * y_local, LANES), jnp.float32),
            pltpu.VMEM((cols, x_full // LANES, z_local * y_local, LANES), jnp.float32),
            pltpu.VMEM(x_table.shape, jnp.bfloat16),
            pltpu.VMEM(z_table.shape, jnp.bfloat16),
            pltpu.VMEM(y_table.shape, jnp.bfloat16),
            pltpu.VMEM((cols, x_full, y_local, LANES), jnp.float32),
            pltpu.VMEM((devices, 2, y_local * SUBLANES, LANES), jnp.float32),
            pltpu.VMEM((cols, 2, y_full * SUBLANES, LANES), jnp.float32),
            pltpu.VMEM((2, y_full // LANES, z_full * SUBLANES, LANES), jnp.float32),
            pltpu.SemaphoreType.DMA(((cols + 1) * (x_full // LANES) + 3,)),
            pltpu.SemaphoreType.DMA((2 + y_full // LANES,)),
            pltpu.SemaphoreType.DMA((devices,)),
            pltpu.SemaphoreType.DMA((devices,)),
            pltpu.SemaphoreType.DMA((devices,)),
            pltpu.SemaphoreType.DMA((devices,)),
        ],
        compiler_params=pltpu.CompilerParams(
            collective_id=0, has_side_effects=True, vmem_limit_bytes=56 * 1024 * 1024
        ),
        cost_estimate=pl.CostEstimate(flops=flops, bytes_accessed=16 * coefficients.size, transcendentals=0),
    )(
        coefficients.reshape(2, z_local * y_local, x_full),
        real_bands.reshape(cols, z_local * y_local, x_full),
        jnp.asarray(x_table),
        jnp.asarray(z_table),
        jnp.asarray(y_table),
    )
    return out.reshape(2, 1, z_full, SUBLANES, y_full), table[None]


def local(coefficients, real_bands):
    rows = lax.axis_size("row")
    cols = lax.axis_size("col")
    _, bands, z_local, y_local, x_full = coefficients.shape
    fits = (
        bands == 1
        and real_bands.shape[0] == cols
        and z_local == LANES
        and y_local % (2 * SUBLANES) == 0
        and x_full == SUBLANES * rows * cols
        and x_full % (2 * LANES) == 0
        and rows % 2 == 0
    )
    if fits:
        return fused(coefficients, real_bands, rows, cols)
    return general(coefficients, real_bands)


def general(coefficients, real_bands):
    rows = lax.axis_size("row")
    cols = lax.axis_size("col")
    devices = rows * cols
    _, bands, z_local, y_local, x_full = coefficients.shape
    z_full = z_local * cols
    y_full = y_local * rows
    x_final = x_full // devices
    table_bands = real_bands.shape[0] // cols
    x_rows = x_full // rows

    turned = real_bands.reshape(cols, table_bands, z_local, y_local, rows, x_rows)
    turned = jnp.transpose(turned, (4, 0, 1, 5, 3, 2))
    turned = turned.reshape(devices, table_bands, x_rows, y_local, z_local)
    placed = lax.all_to_all(turned, axes, split_axis=0, concat_axis=0, tiled=True)
    placed = placed.reshape(rows, cols, table_bands, x_rows, y_local, z_local)
    spline_table = jnp.transpose(placed, (2, 3, 0, 4, 1, 5)).reshape(table_bands, x_rows, y_full, z_full)

    x_table = transform_table(x_full).reshape(2, x_full, 2, devices, x_final)
    z_table = transform_table(z_full).reshape(2, cols, z_local, 2, z_full)
    y_table = transform_table(y_full).reshape(2, rows, y_local, 2, y_full)
    first = jnp.einsum("cbzyk,ckedq->debyqz", coefficients, x_table, precision=precision)
    moved = lax.all_to_all(first, axes, split_axis=0, concat_axis=0, tiled=True)
    moved = moved.reshape(rows, cols, 2, bands, y_local, x_final, z_local)
    second = jnp.einsum("rjebyqz,ejzfn->fbnqry", moved, z_table, precision=precision)
    spline_coefs = jnp.einsum("fbnqry,fryhk->hbnqk", second, y_table, precision=precision)
    return spline_coefs, spline_table


def solution(mesh):
    placed = (P(None, None, "col", "row", None), P(None, "col", "row", None))
    return jax.shard_map(
        local,
        mesh=mesh,
        in_specs=placed,
        out_specs=(P(None, None, None, ("row", "col"), None), P("col", "row", None, None)),
        check_vma=False,
    )
```

```python
import functools
import math

import jax
import jax.numpy as jnp
import ml_dtypes
import numpy as np
from jax import lax
from jax.experimental import pallas as pl
from jax.experimental.pallas import tpu as pltpu
from jax.sharding import PartitionSpec as P

precision = lax.Precision.HIGH
axes = ("row", "col")
MESH = pl.DeviceIdType.MESH
LANES = 128
SUBLANES = 8


def transform_table(length):
    counter = np.arange(length)
    angle = (counter[:, None] * counter[None, :] % length) * (2.0 * math.pi / length)
    weight = 6.0 / ((4.0 + 2.0 * np.cos(counter * (2.0 * math.pi / length))) * math.sqrt(length))
    cosine = np.cos(angle) * weight[:, None]
    sine = np.sin(angle) * weight[:, None]
    table = np.stack([np.stack([cosine, sine], 1), np.stack([-sine, cosine], 1)])
    return table.astype(np.float32)


def split_table(table):
    high = table.astype(ml_dtypes.bfloat16)
    low = (table - high.astype(np.float32)).astype(ml_dtypes.bfloat16)
    return np.stack([high, low])


def split(values):
    high = values.astype(jnp.bfloat16)
    return high, (values - high.astype(jnp.float32)).astype(jnp.bfloat16)


def product(left, right, contract):
    def one(a, b):
        return lax.dot_general(a, b, (contract, ((), ())), preferred_element_type=jnp.float32)

    return one(left[0], right[0]) + (one(left[0], right[1]) + one(left[1], right[0]))


def kernel(
    rows, cols, y_local,
    coefficients, bands, x_table, z_table, y_table,
    out, table_out,
    source, band_in, x_parts, z_parts, y_parts, turned, first, arrived, result,
    load_sem, local_sem, first_send, first_recv, band_send, band_recv,
):
    row, col = lax.axis_index("row"), lax.axis_index("col")
    half_rows = rows // 2
    half, place = row // half_rows, row % half_rows
    x_tiles, y_tiles = source.shape[1], result.shape[1]
    x_full = x_tiles * LANES
    x_rows = x_full // rows
    y_full = y_local * rows
    z_full = LANES * cols
    block = y_local * SUBLANES

    def target(by_col, by_half, step):
        to_row = (half + by_half) % 2 * half_rows + (place + step) % half_rows
        return to_row, (col + by_col) % cols

    def origin(by_col, by_half, step):
        from_row = (half + by_half) % 2 * half_rows + (place - step + half_rows) % half_rows
        return from_row, (col - by_col + cols) % cols

    def number(by_col, by_half, step):
        return (by_col * 2 + by_half) * half_rows + step

    groups = [(by_col, by_half) for by_col in range(cols) for by_half in (1, 0)]

    def each_step(chosen, do):
        def body(step, _):
            for group in chosen:
                if group == (0, 0):
                    pl.when(step > 0)(functools.partial(do, *group, step))
                else:
                    do(*group, step)
            return 0

        lax.fori_loop(0, half_rows, body, 0)

    barrier = pltpu.get_barrier_semaphore()

    def greet(by_col, by_half, step):
        pl.semaphore_signal(barrier, inc=1, device_id=target(by_col, by_half, step), device_id_type=MESH)

    each_step(groups, greet)

    def load(k, src, dst):
        return pltpu.make_async_copy(src, dst, load_sem.at[k])

    half_tiles = x_tiles // 2

    def lead(by_half):
        return (half + by_half) % 2 * half_tiles

    def load_bands(by_col, by_half):
        b = (col + by_col) % cols
        made = []
        for at in range(half_tiles):
            tile = lead(by_half) + at
            lanes = pl.ds(pl.multiple_of(tile * LANES, LANES), LANES)
            made.append(load((by_col * 2 + by_half) * half_tiles + at, bands.at[b, :, lanes], band_in.at[b, tile]))
        return made

    k = cols * x_tiles
    loads = [
        load(k, x_table, x_parts),
        load(k + 1, z_table, z_parts),
        load(k + 2, y_table, y_parts),
    ]
    for tile in range(x_tiles):
        loads.append(load(k + 3 + tile, coefficients.at[:, :, pl.ds(tile * LANES, LANES)], source.at[:, tile]))
    for group in groups[:2]:
        for one in load_bands(*group):
            one.start()
    for one in loads:
        one.start()
    for group in groups[2:]:
        for one in load_bands(*group):
            one.start()

    def turn(by_col, by_half):
        b = (col + by_col) % cols
        first_tile = lead(by_half)
        flat = turned.reshape(cols, x_full * y_local, LANES)

        def body(y, _):
            for at in range(half_tiles):
                plane = band_in[b, first_tile + at, pl.ds(y, LANES, stride=y_local), :]
                flat[b, pl.ds((first_tile + at) * LANES * y_local + y, LANES, stride=y_local), :] = plane.T
            return 0

        lax.fori_loop(0, y_local, body, 0)

    def band_copy(by_col, by_half, step, place_row, place_col):
        k = number(by_col, by_half, step)
        to_row, to_col = target(by_col, by_half, step)
        return pltpu.make_async_remote_copy(
            src_ref=turned.at[to_col, pl.ds(to_row * x_rows, x_rows)],
            dst_ref=table_out.at[
                :,
                pl.ds(pl.multiple_of(place_row * y_local, SUBLANES), y_local),
                pl.ds(pl.multiple_of(place_col * LANES, LANES), LANES),
            ],
            send_sem=band_send.at[k],
            recv_sem=band_recv.at[k],
            device_id=(to_row, to_col),
            device_id_type=MESH,
        )

    def first_copy(by_col, by_half, step, place_row, place_col):
        k = number(by_col, by_half, step)
        to_row, to_col = target(by_col, by_half, step)
        return pltpu.make_async_remote_copy(
            src_ref=first.at[to_row * cols + to_col],
            dst_ref=arrived.at[place_col, :, pl.ds(pl.multiple_of(place_row * block, SUBLANES), block)],
            send_sem=first_send.at[k],
            recv_sem=first_recv.at[k],
            device_id=(to_row, to_col),
            device_id_type=MESH,
        )

    def send_band(by_col, by_half, step):
        band_copy(by_col, by_half, step, row, col).start()

    for one in load_bands(0, 1):
        one.wait()
    turn(0, 1)
    pl.semaphore_wait(barrier, rows * cols - 1)
    each_step([(0, 1)], send_band)
    for one in load_bands(0, 0):
        one.wait()
    turn(0, 0)
    each_step([(0, 0)], send_band)

    for one in loads:
        one.wait()

    def x_step(pair, _):
        y = pair * 2
        parts = []
        for part in range(2):
            for tile in range(x_tiles):
                lines = [source[part, tile, pl.ds(y + j, LANES, stride=y_local), :] for j in range(2)]
                parts.append(jnp.concatenate(lines, axis=0))
        lines = split(jnp.concatenate(parts, axis=1))
        made = product((x_parts[0], x_parts[1]), lines, ((1,), (1,)))
        for part in range(2):
            for j in range(2):
                piece = made[part * x_full : (part + 1) * x_full, j * LANES : (j + 1) * LANES]
                at = pl.multiple_of((y + j) * SUBLANES, SUBLANES)
                first[:, part, pl.ds(at, SUBLANES), :] = piece.reshape(rows * cols, SUBLANES, LANES)
        return 0

    lax.fori_loop(0, y_local // 2, x_step, 0)

    each_step(groups, lambda *at: first_copy(*at, row, col).start())
    own_first = pltpu.make_async_copy(
        first.at[row * cols + col],
        arrived.at[col, :, pl.ds(pl.multiple_of(row * block, SUBLANES), block)],
        local_sem.at[0],
    )
    own_first.start()

    for group in groups[2:]:
        for one in load_bands(*group):
            one.wait()
        turn(*group)

    def send_rest(step, _):
        for group in groups:

            def sent(group=group):
                first_copy(*group, step, *origin(*group, step)).wait_send()

            if group == (0, 0):
                pl.when(step > 0)(sent)
            else:
                sent()
        for group in groups[2:]:
            send_band(*group, step)
        return 0

    lax.fori_loop(0, half_rows, send_rest, 0)
    own_band = pltpu.make_async_copy(
        turned.at[col, pl.ds(row * x_rows, x_rows)],
        table_out.at[
            :,
            pl.ds(pl.multiple_of(row * y_local, SUBLANES), y_local),
            pl.ds(pl.multiple_of(col * LANES, LANES), LANES),
        ],
        local_sem.at[1],
    )
    own_band.start()

    own_first.wait()
    each_step(groups, lambda *at: first_copy(*at, *origin(*at)).wait_recv())

    def final_step(x, _):
        pieces = [
            arrived[c, part, pl.ds(x, y_full, stride=SUBLANES), :] for part in range(2) for c in range(cols)
        ]
        lines = split(jnp.concatenate(pieces, axis=1))
        second = product((z_parts[0], z_parts[1]), lines, ((1,), (1,)))
        lines = split(jnp.concatenate([second[:z_full], second[z_full:]], axis=1))
        third = product(lines, (y_parts[0], y_parts[1]), ((1,), (0,)))
        for part in range(2):
            for tile in range(y_tiles):
                at = part * y_full + tile * LANES
                result[part, tile, pl.ds(x, z_full, stride=SUBLANES), :] = third[:, at : at + LANES]
        return 0

    lax.fori_loop(0, SUBLANES, final_step, 0)
    stores = [
        pltpu.make_async_copy(result.at[:, tile], out.at[:, :, pl.ds(tile * LANES, LANES)], local_sem.at[2 + tile])
        for tile in range(y_tiles)
    ]
    for store in stores:
        store.start()
    for store in stores:
        store.wait()
    own_band.wait()
    each_step(groups, lambda *at: band_copy(*at, *origin(*at)).wait_send())
    each_step(groups, lambda *at: band_copy(*at, *origin(*at)).wait_recv())


def fused(coefficients, real_bands, rows, cols):
    _, _, z_local, y_local, x_full = coefficients.shape
    z_full, y_full, devices = z_local * cols, y_local * rows, rows * cols
    x_rows = x_full // rows
    x_table = split_table(np.transpose(transform_table(x_full), (2, 3, 0, 1)).reshape(2 * x_full, 2 * x_full))
    z_table = split_table(np.transpose(transform_table(z_full), (2, 3, 0, 1)).reshape(2 * z_full, 2 * z_full))
    y_table = split_table(transform_table(y_full).reshape(2 * y_full, 2 * y_full))
    flops = 3 * 2 * 2 * 2 * (x_full + y_full + z_full) * coefficients.size
    out, table = pl.pallas_call(
        functools.partial(kernel, rows, cols, y_local),
        out_shape=[
            pltpu.VMEM((2, z_full * SUBLANES, y_full), jnp.float32),
            pltpu.VMEM((x_rows, y_full, z_full), jnp.float32),
        ],
        in_specs=[pl.BlockSpec(memory_space=pl.ANY)] * 5,
        out_specs=[pl.BlockSpec(memory_space=pltpu.VMEM)] * 2,
        scratch_shapes=[
            pltpu.VMEM((2, x_full // LANES, z_local * y_local, LANES), jnp.float32),
            pltpu.VMEM((cols, x_full // LANES, z_local * y_local, LANES), jnp.float32),
            pltpu.VMEM(x_table.shape, jnp.bfloat16),
            pltpu.VMEM(z_table.shape, jnp.bfloat16),
            pltpu.VMEM(y_table.shape, jnp.bfloat16),
            pltpu.VMEM((cols, x_full, y_local, LANES), jnp.float32),
            pltpu.VMEM((devices, 2, y_local * SUBLANES, LANES), jnp.float32),
            pltpu.VMEM((cols, 2, y_full * SUBLANES, LANES), jnp.float32),
            pltpu.VMEM((2, y_full // LANES, z_full * SUBLANES, LANES), jnp.float32),
            pltpu.SemaphoreType.DMA(((cols + 1) * (x_full // LANES) + 3,)),
            pltpu.SemaphoreType.DMA((2 + y_full // LANES,)),
            pltpu.SemaphoreType.DMA((devices,)),
            pltpu.SemaphoreType.DMA((devices,)),
            pltpu.SemaphoreType.DMA((devices,)),
            pltpu.SemaphoreType.DMA((devices,)),
        ],
        compiler_params=pltpu.CompilerParams(
            collective_id=0, has_side_effects=True, vmem_limit_bytes=40 * 1024 * 1024
        ),
        cost_estimate=pl.CostEstimate(flops=flops, bytes_accessed=16 * coefficients.size, transcendentals=0),
    )(
        coefficients.reshape(2, z_local * y_local, x_full),
        real_bands.reshape(cols, z_local * y_local, x_full),
        jnp.asarray(x_table),
        jnp.asarray(z_table),
        jnp.asarray(y_table),
    )
    return out.reshape(2, 1, z_full, SUBLANES, y_full), table[None]


def local(coefficients, real_bands):
    rows = lax.axis_size("row")
    cols = lax.axis_size("col")
    _, bands, z_local, y_local, x_full = coefficients.shape
    fits = (
        bands == 1
        and real_bands.shape[0] == cols
        and z_local == LANES
        and y_local % (2 * SUBLANES) == 0
        and x_full == SUBLANES * rows * cols
        and x_full % (2 * LANES) == 0
        and rows % 2 == 0
    )
    if fits:
        return fused(coefficients, real_bands, rows, cols)
    return general(coefficients, real_bands)


def general(coefficients, real_bands):
    rows = lax.axis_size("row")
    cols = lax.axis_size("col")
    devices = rows * cols
    _, bands, z_local, y_local, x_full = coefficients.shape
    z_full = z_local * cols
    y_full = y_local * rows
    x_final = x_full // devices
    table_bands = real_bands.shape[0] // cols
    x_rows = x_full // rows

    turned = real_bands.reshape(cols, table_bands, z_local, y_local, rows, x_rows)
    turned = jnp.transpose(turned, (4, 0, 1, 5, 3, 2))
    turned = turned.reshape(devices, table_bands, x_rows, y_local, z_local)
    placed = lax.all_to_all(turned, axes, split_axis=0, concat_axis=0, tiled=True)
    placed = placed.reshape(rows, cols, table_bands, x_rows, y_local, z_local)
    spline_table = jnp.transpose(placed, (2, 3, 0, 4, 1, 5)).reshape(table_bands, x_rows, y_full, z_full)

    x_table = transform_table(x_full).reshape(2, x_full, 2, devices, x_final)
    z_table = transform_table(z_full).reshape(2, cols, z_local, 2, z_full)
    y_table = transform_table(y_full).reshape(2, rows, y_local, 2, y_full)
    first = jnp.einsum("cbzyk,ckedq->debyqz", coefficients, x_table, precision=precision)
    moved = lax.all_to_all(first, axes, split_axis=0, concat_axis=0, tiled=True)
    moved = moved.reshape(rows, cols, 2, bands, y_local, x_final, z_local)
    second = jnp.einsum("rjebyqz,ejzfn->fbnqry", moved, z_table, precision=precision)
    spline_coefs = jnp.einsum("fbnqry,fryhk->hbnqk", second, y_table, precision=precision)
    return spline_coefs, spline_table


def solution(mesh):
    placed = (P(None, None, "col", "row", None), P(None, "col", "row", None))
    return jax.shard_map(
        local,
        mesh=mesh,
        in_specs=placed,
        out_specs=(P(None, None, None, ("row", "col"), None), P("col", "row", None, None)),
        check_vma=False,
    )
```

```python
import functools
import math

import jax
import jax.numpy as jnp
import ml_dtypes
import numpy as np
from jax import lax
from jax.experimental import pallas as pl
from jax.experimental.pallas import tpu as pltpu
from jax.sharding import PartitionSpec as P

precision = lax.Precision.HIGH
axes = ("row", "col")
MESH = pl.DeviceIdType.MESH
LANES = 128
SUBLANES = 8


def transform_table(length):
    counter = np.arange(length)
    angle = (counter[:, None] * counter[None, :] % length) * (2.0 * math.pi / length)
    weight = 6.0 / ((4.0 + 2.0 * np.cos(counter * (2.0 * math.pi / length))) * math.sqrt(length))
    cosine = np.cos(angle) * weight[:, None]
    sine = np.sin(angle) * weight[:, None]
    table = np.stack([np.stack([cosine, sine], 1), np.stack([-sine, cosine], 1)])
    return table.astype(np.float32)


def split_table(table):
    high = table.astype(ml_dtypes.bfloat16)
    low = (table - high.astype(np.float32)).astype(ml_dtypes.bfloat16)
    return np.stack([high, low])


def split(values):
    high = values.astype(jnp.bfloat16)
    return high, (values - high.astype(jnp.float32)).astype(jnp.bfloat16)


def product(left, right, contract):
    def one(a, b):
        return lax.dot_general(a, b, (contract, ((), ())), preferred_element_type=jnp.float32)

    return one(left[0], right[0]) + (one(left[0], right[1]) + one(left[1], right[0]))


def kernel(
    rows, cols, y_local,
    coefficients, bands, x_table, z_table, y_table,
    out, table_out,
    source, band_in, x_parts, z_parts, y_parts, turned, first, arrived, result,
    load_sem, local_sem, first_send, first_recv, band_send, band_recv,
):
    row, col = lax.axis_index("row"), lax.axis_index("col")
    half_rows = rows // 2
    half, place = row // half_rows, row % half_rows
    x_tiles, y_tiles = source.shape[1], result.shape[1]
    x_full = x_tiles * LANES
    x_rows = x_full // rows
    y_full = y_local * rows
    z_full = LANES * cols
    block = y_local * SUBLANES

    def target(by_col, by_half, step):
        to_row = (half + by_half) % 2 * half_rows + (place + step) % half_rows
        return to_row, (col + by_col) % cols

    def origin(by_col, by_half, step):
        from_row = (half + by_half) % 2 * half_rows + (place - step + half_rows) % half_rows
        return from_row, (col - by_col + cols) % cols

    def number(by_col, by_half, step):
        return (by_col * 2 + by_half) * half_rows + step

    groups = [(by_col, by_half) for by_col in range(cols) for by_half in (1, 0)]

    def each_step(chosen, do):
        def body(step, _):
            for group in chosen:
                if group == (0, 0):
                    pl.when(step > 0)(functools.partial(do, *group, step))
                else:
                    do(*group, step)
            return 0

        lax.fori_loop(0, half_rows, body, 0)

    phase = place % 2

    def each_turn(chosen, do):
        def body(step, _):
            for by_col, by_half in chosen:
                by_half = (by_half + phase) % 2
                if by_col == 0:
                    pl.when(by_half + step > 0)(functools.partial(do, by_col, by_half, step))
                else:
                    do(by_col, by_half, step)
            return 0

        lax.fori_loop(0, half_rows, body, 0)

    barrier = pltpu.get_barrier_semaphore()

    def greet(by_col, by_half, step):
        pl.semaphore_signal(barrier, inc=1, device_id=target(by_col, by_half, step), device_id_type=MESH)

    each_step(groups, greet)

    def load(k, src, dst):
        return pltpu.make_async_copy(src, dst, load_sem.at[k])

    half_tiles = x_tiles // 2

    def lead(by_half):
        return (half + by_half) % 2 * half_tiles

    def load_bands(by_col, by_half):
        b = (col + by_col) % cols
        made = []
        for at in range(half_tiles):
            tile = lead(by_half) + at
            lanes = pl.ds(pl.multiple_of(tile * LANES, LANES), LANES)
            made.append(load((by_col * 2 + by_half) * half_tiles + at, bands.at[b, :, lanes], band_in.at[b, tile]))
        return made

    k = cols * x_tiles
    loads = [
        load(k, x_table, x_parts),
        load(k + 1, z_table, z_parts),
        load(k + 2, y_table, y_parts),
    ]
    for tile in range(x_tiles):
        loads.append(load(k + 3 + tile, coefficients.at[:, :, pl.ds(tile * LANES, LANES)], source.at[:, tile]))
    for by_col, by_half in groups[:2]:
        for one in load_bands(by_col, (by_half + phase) % 2):
            one.start()
    for one in loads:
        one.start()
    for group in groups[2:]:
        for one in load_bands(*group):
            one.start()

    def turn(by_col, by_half):
        b = (col + by_col) % cols
        first_tile = lead(by_half)
        flat = turned.reshape(cols, x_full * y_local, LANES)

        def body(y, _):
            for at in range(half_tiles):
                plane = band_in[b, first_tile + at, pl.ds(y, LANES, stride=y_local), :]
                flat[b, pl.ds((first_tile + at) * LANES * y_local + y, LANES, stride=y_local), :] = plane.T
            return 0

        lax.fori_loop(0, y_local, body, 0)

    def band_copy(by_col, by_half, step, place_row, place_col):
        k = number(by_col, by_half, step)
        to_row, to_col = target(by_col, by_half, step)
        return pltpu.make_async_remote_copy(
            src_ref=turned.at[to_col, pl.ds(to_row * x_rows, x_rows)],
            dst_ref=table_out.at[
                :,
                pl.ds(pl.multiple_of(place_row * y_local, SUBLANES), y_local),
                pl.ds(pl.multiple_of(place_col * LANES, LANES), LANES),
            ],
            send_sem=band_send.at[k],
            recv_sem=band_recv.at[k],
            device_id=(to_row, to_col),
            device_id_type=MESH,
        )

    def first_copy(by_col, by_half, step, place_row, place_col):
        k = number(by_col, by_half, step)
        to_row, to_col = target(by_col, by_half, step)
        return pltpu.make_async_remote_copy(
            src_ref=first.at[to_row * cols + to_col],
            dst_ref=arrived.at[place_col, :, pl.ds(pl.multiple_of(place_row * block, SUBLANES), block)],
            send_sem=first_send.at[k],
            recv_sem=first_recv.at[k],
            device_id=(to_row, to_col),
            device_id_type=MESH,
        )

    def send_band(by_col, by_half, step):
        band_copy(by_col, by_half, step, row, col).start()

    for by_half in (1, 0):
        for one in load_bands(0, (by_half + phase) % 2):
            one.wait()
        turn(0, (by_half + phase) % 2)
        if by_half == 1:
            pl.semaphore_wait(barrier, rows * cols - 1)
        each_turn([(0, by_half)], send_band)

    for one in loads:
        one.wait()

    def x_step(pair, _):
        y = pair * 2
        parts = []
        for part in range(2):
            for tile in range(x_tiles):
                lines = [source[part, tile, pl.ds(y + j, LANES, stride=y_local), :] for j in range(2)]
                parts.append(jnp.concatenate(lines, axis=0))
        lines = split(jnp.concatenate(parts, axis=1))
        made = product((x_parts[0], x_parts[1]), lines, ((1,), (1,)))
        for part in range(2):
            for j in range(2):
                piece = made[part * x_full : (part + 1) * x_full, j * LANES : (j + 1) * LANES]
                at = pl.multiple_of((y + j) * SUBLANES, SUBLANES)
                first[:, part, pl.ds(at, SUBLANES), :] = piece.reshape(rows * cols, SUBLANES, LANES)
        return 0

    lax.fori_loop(0, y_local // 2, x_step, 0)

    each_turn(groups, lambda *at: first_copy(*at, row, col).start())
    own_first = pltpu.make_async_copy(
        first.at[row * cols + col],
        arrived.at[col, :, pl.ds(pl.multiple_of(row * block, SUBLANES), block)],
        local_sem.at[0],
    )
    own_first.start()

    for group in groups[2:]:
        for one in load_bands(*group):
            one.wait()
        turn(*group)

    each_turn(groups[2:], send_band)
    own_band = pltpu.make_async_copy(
        turned.at[col, pl.ds(row * x_rows, x_rows)],
        table_out.at[
            :,
            pl.ds(pl.multiple_of(row * y_local, SUBLANES), y_local),
            pl.ds(pl.multiple_of(col * LANES, LANES), LANES),
        ],
        local_sem.at[1],
    )
    own_band.start()

    own_first.wait()
    each_step(groups, lambda *at: first_copy(*at, *origin(*at)).wait_recv())

    def final_step(x, _):
        pieces = [
            arrived[c, part, pl.ds(x, y_full, stride=SUBLANES), :] for part in range(2) for c in range(cols)
        ]
        lines = split(jnp.concatenate(pieces, axis=1))
        second = product((z_parts[0], z_parts[1]), lines, ((1,), (1,)))
        lines = split(jnp.concatenate([second[:z_full], second[z_full:]], axis=1))
        third = product(lines, (y_parts[0], y_parts[1]), ((1,), (0,)))
        for part in range(2):
            for tile in range(y_tiles):
                at = part * y_full + tile * LANES
                result[part, tile, pl.ds(x, z_full, stride=SUBLANES), :] = third[:, at : at + LANES]
        return 0

    lax.fori_loop(0, SUBLANES, final_step, 0)
    stores = [
        pltpu.make_async_copy(result.at[:, tile], out.at[:, :, pl.ds(tile * LANES, LANES)], local_sem.at[2 + tile])
        for tile in range(y_tiles)
    ]
    for store in stores:
        store.start()
    for store in stores:
        store.wait()
    own_band.wait()
    each_step(groups, lambda *at: first_copy(*at, *origin(*at)).wait_send())
    each_step(groups, lambda *at: band_copy(*at, *origin(*at)).wait_send())
    each_step(groups, lambda *at: band_copy(*at, *origin(*at)).wait_recv())


def fused(coefficients, real_bands, rows, cols):
    _, _, z_local, y_local, x_full = coefficients.shape
    z_full, y_full, devices = z_local * cols, y_local * rows, rows * cols
    x_rows = x_full // rows
    x_table = split_table(np.transpose(transform_table(x_full), (2, 3, 0, 1)).reshape(2 * x_full, 2 * x_full))
    z_table = split_table(np.transpose(transform_table(z_full), (2, 3, 0, 1)).reshape(2 * z_full, 2 * z_full))
    y_table = split_table(transform_table(y_full).reshape(2 * y_full, 2 * y_full))
    flops = 3 * 2 * 2 * 2 * (x_full + y_full + z_full) * coefficients.size
    out, table = pl.pallas_call(
        functools.partial(kernel, rows, cols, y_local),
        out_shape=[
            pltpu.VMEM((2, z_full * SUBLANES, y_full), jnp.float32),
            pltpu.VMEM((x_rows, y_full, z_full), jnp.float32),
        ],
        in_specs=[pl.BlockSpec(memory_space=pl.ANY)] * 5,
        out_specs=[pl.BlockSpec(memory_space=pltpu.VMEM)] * 2,
        scratch_shapes=[
            pltpu.VMEM((2, x_full // LANES, z_local * y_local, LANES), jnp.float32),
            pltpu.VMEM((cols, x_full // LANES, z_local * y_local, LANES), jnp.float32),
            pltpu.VMEM(x_table.shape, jnp.bfloat16),
            pltpu.VMEM(z_table.shape, jnp.bfloat16),
            pltpu.VMEM(y_table.shape, jnp.bfloat16),
            pltpu.VMEM((cols, x_full, y_local, LANES), jnp.float32),
            pltpu.VMEM((devices, 2, y_local * SUBLANES, LANES), jnp.float32),
            pltpu.VMEM((cols, 2, y_full * SUBLANES, LANES), jnp.float32),
            pltpu.VMEM((2, y_full // LANES, z_full * SUBLANES, LANES), jnp.float32),
            pltpu.SemaphoreType.DMA(((cols + 1) * (x_full // LANES) + 3,)),
            pltpu.SemaphoreType.DMA((2 + y_full // LANES,)),
            pltpu.SemaphoreType.DMA((devices,)),
            pltpu.SemaphoreType.DMA((devices,)),
            pltpu.SemaphoreType.DMA((devices,)),
            pltpu.SemaphoreType.DMA((devices,)),
        ],
        compiler_params=pltpu.CompilerParams(
            collective_id=0, has_side_effects=True, vmem_limit_bytes=55 * 1024 * 1024
        ),
        cost_estimate=pl.CostEstimate(flops=flops, bytes_accessed=16 * coefficients.size, transcendentals=0),
    )(
        coefficients.reshape(2, z_local * y_local, x_full),
        real_bands.reshape(cols, z_local * y_local, x_full),
        jnp.asarray(x_table),
        jnp.asarray(z_table),
        jnp.asarray(y_table),
    )
    return out.reshape(2, 1, z_full, SUBLANES, y_full), table[None]


def local(coefficients, real_bands):
    rows = lax.axis_size("row")
    cols = lax.axis_size("col")
    _, bands, z_local, y_local, x_full = coefficients.shape
    fits = (
        bands == 1
        and real_bands.shape[0] == cols
        and z_local == LANES
        and y_local % (2 * SUBLANES) == 0
        and x_full == SUBLANES * rows * cols
        and x_full % (2 * LANES) == 0
        and rows % 2 == 0
    )
    if fits:
        return fused(coefficients, real_bands, rows, cols)
    return general(coefficients, real_bands)


def general(coefficients, real_bands):
    rows = lax.axis_size("row")
    cols = lax.axis_size("col")
    devices = rows * cols
    _, bands, z_local, y_local, x_full = coefficients.shape
    z_full = z_local * cols
    y_full = y_local * rows
    x_final = x_full // devices
    table_bands = real_bands.shape[0] // cols
    x_rows = x_full // rows

    turned = real_bands.reshape(cols, table_bands, z_local, y_local, rows, x_rows)
    turned = jnp.transpose(turned, (4, 0, 1, 5, 3, 2))
    turned = turned.reshape(devices, table_bands, x_rows, y_local, z_local)
    placed = lax.all_to_all(turned, axes, split_axis=0, concat_axis=0, tiled=True)
    placed = placed.reshape(rows, cols, table_bands, x_rows, y_local, z_local)
    spline_table = jnp.transpose(placed, (2, 3, 0, 4, 1, 5)).reshape(table_bands, x_rows, y_full, z_full)

    x_table = transform_table(x_full).reshape(2, x_full, 2, devices, x_final)
    z_table = transform_table(z_full).reshape(2, cols, z_local, 2, z_full)
    y_table = transform_table(y_full).reshape(2, rows, y_local, 2, y_full)
    first = jnp.einsum("cbzyk,ckedq->debyqz", coefficients, x_table, precision=precision)
    moved = lax.all_to_all(first, axes, split_axis=0, concat_axis=0, tiled=True)
    moved = moved.reshape(rows, cols, 2, bands, y_local, x_final, z_local)
    second = jnp.einsum("rjebyqz,ejzfn->fbnqry", moved, z_table, precision=precision)
    spline_coefs = jnp.einsum("fbnqry,fryhk->hbnqk", second, y_table, precision=precision)
    return spline_coefs, spline_table


def solution(mesh):
    placed = (P(None, None, "col", "row", None), P(None, "col", "row", None))
    return jax.shard_map(
        local,
        mesh=mesh,
        in_specs=placed,
        out_specs=(P(None, None, None, ("row", "col"), None), P("col", "row", None, None)),
        check_vma=False,
    )
```
